256 devices in a mesh: row: 16 (over x_lo, z), col: 16 (over x_hi, y, core).
Axes of the slice: x: 4 (x_hi: 2, x_lo: 2; x = x_hi * 2 + x_lo), y: 4, z: 8, core: 2. Of those that a mesh axis runs over, the one named last changes fastest.
Arguments:
- queries: bfloat16 [192, 512, 2048], P('row', 'col'), may hold values from -192 to 192
- key_vectors: bfloat16 [192, 512, 2048], P('row', 'col'), may hold values from -6 to 6
- value_vectors: bfloat16 [192, 512, 2048], P('row', 'col'), may hold values from -6 to 6
- grad_output: bfloat16 [192, 512, 2048], P('row', 'col'), may hold values from -6 to 6
Outputs:
- grad_queries: bfloat16 [192, 512, 2048], P('row', 'col')
- grad_keys: bfloat16 [192, 512, 2048], P('row', 'col')
- grad_values: bfloat16 [192, 512, 2048], P('row', 'col')
The draws below stay inside these ranges and needn't reach their ends.
All inputs are finite; a program needn't handle non-finite values.
Results may differ from the reference program's by a relative error of at most 0.012.
The reference program's roundings to bfloat16 on the way count: a program that leaves them out, or rounds other values in their place, can miss the bound.
Values may be sent and summed in bfloat16 or wider, within the bound.
A program may use at most 128 MiB of HBM per device.

```python
import math
import jax
import jax.numpy as jnp
from jax import lax

D = 2048
HEADS = 16
HEAD_DIM = 128
ROWS = 192
COLS = 512


def shared_keys(key):
    return jnp.clip(jax.random.normal(key, (ROWS, COLS, D), jnp.float32), -6.0, 6.0)


def draw_key_vectors(key, part):
    base = shared_keys(key)
    return base.astype(jnp.bfloat16)


def draw_queries(key, part):
    key = jax.random.fold_in(key, 5)
    noise = jnp.clip(jax.random.normal(key, (ROWS, COLS, D), jnp.float32), -6.0, 6.0)
    return noise.astype(jnp.bfloat16)


def steps_of(stream_key, extent, shards, low, top_value):
    factor_of = 1.0
    for axis_at, shards_of in shards:
        draws = jax.random.uniform(jax.random.fold_in(jax.random.fold_in(stream_key, 6), axis_at), (shards_of,), jnp.float32, low / len(shards), top_value / len(shards))
        factor_of = factor_of * jnp.repeat(jnp.exp(draws), extent[axis_at] // shards_of).reshape((-1,) + (1,) * (len(extent) - 1 - axis_at))
    return factor_of


def centred(rng, shape, width, bound, pieces=(), kind=jnp.bfloat16):
    values = width * jax.random.normal(rng, shape, jnp.float32)
    if pieces:
        values = values * steps_of(rng, shape, pieces, -0.22, 0.18)
    return jnp.clip(values, -bound, bound).astype(kind)


def setup_inputs(seed: int = 0) -> dict:
    key_list = jax.random.split(jax.random.key(seed), 5)
    return {
        "queries": draw_queries(jax.random.fold_in(key_list[4], 71), 0),
        "key_vectors": draw_key_vectors(jax.random.fold_in(key_list[4], 71), 0),
        "value_vectors": centred(key_list[2], (ROWS, COLS, D), 1.0, 6.0, ((0, 16), (1, 16))),
        "grad_output": centred(key_list[3], (ROWS, COLS, D), 1.0, 6.0, ((0, 16), (1, 16))),
    }


def attend_back(query_block, key_block, value_block, grad_block):
    length = query_block.shape[1]
    factor = 1.0 / math.sqrt(query_block.shape[2])
    query32 = query_block.astype(jnp.float32)
    key32 = key_block.astype(jnp.float32)
    value32 = value_block.astype(jnp.float32)
    grad32 = grad_block.astype(jnp.float32)
    scores = jnp.einsum('gqe,gke->gqk', query32, key32) * factor
    position = lax.broadcasted_iota(jnp.int32, (length, length), 0)
    column_index = lax.broadcasted_iota(jnp.int32, (length, length), 1)
    scores = jnp.where(column_index <= position, scores, -jnp.inf)
    highest = lax.optimization_barrier(jnp.max(scores, axis=-1, keepdims=True))
    weights = jnp.exp(scores - highest)
    probability = weights / lax.optimization_barrier(jnp.sum(weights, axis=-1, keepdims=True))
    weights_low = lax.optimization_barrier(probability.astype(jnp.bfloat16)).astype(jnp.float32)
    attended = jnp.einsum('gqk,gke->gqe', weights_low, value32)
    correction = lax.optimization_barrier(jnp.sum(grad32 * attended, axis=-1, keepdims=True))
    grad_weights = jnp.einsum('gqe,gke->gqk', grad32, value32)
    grad_scores = lax.optimization_barrier((probability * (grad_weights - correction)).astype(jnp.bfloat16)).astype(jnp.float32)
    grad_value = jnp.einsum('gqk,gqe->gke', weights_low, grad32)
    grad_query = jnp.einsum('gqk,gke->gqe', grad_scores, key32) * factor
    grad_key = jnp.einsum('gqk,gqe->gke', grad_scores, query32) * factor
    return (grad_query.astype(jnp.bfloat16), grad_key.astype(jnp.bfloat16), grad_value.astype(jnp.bfloat16))

def reference(queries, key_vectors, value_vectors, grad_output):
    half_width = D // 2
    heads_half = HEADS // 2

    def row_step(blocks):
        parts = [b[:, :half_width].reshape(COLS, heads_half, HEAD_DIM).transpose(1, 0, 2) for b in blocks]
        return attend_back(parts[0], parts[1], parts[2], parts[3])
    row_results = lax.map(row_step, (queries, key_vectors, value_vectors, grad_output))

    def col_step(index):
        parts = []
        for array in (queries, key_vectors, value_vectors, grad_output):
            column = lax.dynamic_index_in_dim(array, index, 1, keepdims=False)
            parts.append(column[:, half_width:].reshape(ROWS, heads_half, HEAD_DIM).transpose(1, 0, 2))
        return attend_back(parts[0], parts[1], parts[2], parts[3])
    col_results = lax.map(col_step, jnp.arange(COLS, dtype=jnp.int32))
    outputs = []
    for which in range(3):
        row_part = row_results[which].transpose(0, 2, 1, 3).reshape(ROWS, COLS, half_width)
        col_part = col_results[which].transpose(2, 0, 1, 3).reshape(ROWS, COLS, half_width)
        outputs.append(jnp.concatenate([row_part, col_part], axis=2))
    return (outputs[0], outputs[1], outputs[2])
```

```python
import functools
import math

import jax
import jax.numpy as jnp
from jax import lax
from jax.experimental import pallas as pl
from jax.experimental.pallas import tpu as pltpu
from jax.sharding import PartitionSpec as P

MESH = pl.DeviceIdType.MESH
HEAD_DIM = 128
RING = 8
FACTOR = 1.0 / math.sqrt(HEAD_DIM)
LOG2E = math.log2(math.e)
BF16, F32 = jnp.bfloat16, jnp.float32

KEY, VALUE, QUERY, GRAD = range(4)
DKEY, DVALUE, DQUERY = range(3)
COL_CHUNKS = 2
ROW_CHUNKS = 2


def attend_back(keys, values, queries, grads, causal_from):
    key_count, query_count = keys.shape[0], queries.shape[0]
    contract_last = (((1,), (1,)), ((), ()))
    raw = lax.dot_general(keys, queries, contract_last, preferred_element_type=F32)
    key_at = lax.broadcasted_iota(jnp.int32, (key_count, query_count), 0)
    query_at = lax.broadcasted_iota(jnp.int32, (key_count, query_count), 1)
    raw = jnp.where(key_at <= query_at + causal_from, raw, -jnp.inf)
    highest = jnp.max(raw, axis=0, keepdims=True)
    weights = jnp.exp2((raw - highest) * (FACTOR * LOG2E))
    probs = weights * (1.0 / jnp.sum(weights, axis=0, keepdims=True))
    probs_low = probs.astype(BF16)
    grad_weights = lax.dot_general(values, grads, contract_last, preferred_element_type=F32)
    correction = jnp.sum(probs_low.astype(F32) * grad_weights, axis=0, keepdims=True)
    grad_scores = (probs * (grad_weights - correction)).astype(BF16)
    grad_values = jnp.dot(probs_low, grads, preferred_element_type=F32)
    grad_keys = jnp.dot(grad_scores, queries, preferred_element_type=F32) * FACTOR
    grad_queries = (
        lax.dot_general(grad_scores, keys, (((0,), (0,)), ((), ())), preferred_element_type=F32)
        * FACTOR
    )
    return grad_keys, grad_values, grad_queries


def kernel(
    q_ref, k_ref, v_ref, g_ref, dq_ref, dk_ref, dv_ref,
    c_in, c_low, c_out, c_part, c_back, f_in, f_out,
    r_in, r_low, r_out, r_part, r_back, r_sum,
    ci_send, ci_recv, cl_send, cl_recv, cb_send, cb_recv, co_send, co_recv,
    ri_send, ri_recv, rl_send, rl_recv, rb_send, rb_recv, ro_send, ro_recv,
):
    inputs = (k_ref, v_ref, q_ref, g_ref)
    outputs = (dk_ref, dv_ref, dq_ref)
    row_count, col_count, width = q_ref.shape
    half = width // 2
    col_step = col_count // COL_CHUNKS
    row_step = row_count // ROW_CHUNKS
    col_len = row_count * RING
    row_len = col_count * RING

    row = lax.axis_index("row")
    col = lax.axis_index("col")
    x_lo, z = row // RING, lax.rem(row, RING)
    x_hi, j = col // RING, lax.rem(col, RING)

    def z_peer(at):
        return (x_lo * RING + at, col)

    def j_peer(at):
        return (row, x_hi * RING + at)

    lo_peer = ((1 - x_lo) * RING + z, col)
    hi_peer = (row, (1 - x_hi) * RING + j)

    def others(start, step):
        def at(d, carry):
            step(lax.rem(start + d, RING))
            return carry

        lax.fori_loop(1, RING, at, 0)

    barrier = pltpu.get_barrier_semaphore()

    def greet(target):
        pl.semaphore_signal(barrier, inc=1, device_id=target, device_id_type=MESH)

    others(z, lambda at: greet(z_peer(at)))
    others(j, lambda at: greet(j_peer(at)))
    greet(lo_peer)
    greet(hi_peer)
    pl.semaphore_wait(barrier, 2 * RING)

    def lanes(first):
        return pl.ds(pl.multiple_of(first, HEAD_DIM), HEAD_DIM)

    def send(src, dst, send_sem, recv_sem, target):
        pltpu.make_async_remote_copy(
            src_ref=src, dst_ref=dst, send_sem=send_sem, recv_sem=recv_sem,
            device_id=target, device_id_type=MESH,
        ).start()

    def take(ref, sem):
        pltpu.make_async_copy(ref, ref, sem).wait()

    def c_rows(at):
        return pl.ds(at * row_count, row_count)

    def r_cols(at):
        return pl.ds(pl.multiple_of(at * col_count, col_count), col_count)

    def c_send_in(t, n):
        def src(at):
            return inputs[t].at[:, pl.ds(n * col_step, col_step), lanes(half + at * HEAD_DIM)]

        dst = c_in.at[t, n, c_rows(z)]
        others(z, lambda at: send(src(at), dst, ci_send.at[t, n], ci_recv.at[t, n], z_peer(at)))
        pltpu.make_async_copy(src(z), dst, ci_recv.at[t, n]).start()

    def c_send_out(o, n):
        dst = outputs[o].at[:, pl.ds(n * col_step, col_step), lanes(half + z * HEAD_DIM)]

        def src(at):
            return c_out.at[o, n, c_rows(at)]

        others(z, lambda at: send(src(at), dst, co_send.at[o, n], co_recv.at[o, n], z_peer(at)))
        pltpu.make_async_copy(src(z), dst, co_recv.at[o, n]).start()

    def r_span(n):
        return pl.ds(n * row_step, row_step)

    def r_send_in(t, n):
        def src(at):
            return inputs[t].at[r_span(n), :, lanes(at * HEAD_DIM)]

        dst = r_in.at[t, r_span(n), r_cols(j)]
        others(j, lambda at: send(src(at), dst, ri_send.at[t, n], ri_recv.at[t, n], j_peer(at)))
        pltpu.make_async_copy(src(j), dst, ri_recv.at[t, n]).start()

    def r_send_out(o, n):
        dst = outputs[o].at[r_span(n), :, lanes(j * HEAD_DIM)]

        def src(at):
            return r_out.at[o, r_span(n), r_cols(at)]

        others(j, lambda at: send(src(at), dst, ro_send.at[o, n], ro_recv.at[o, n], j_peer(at)))
        pltpu.make_async_copy(src(j), dst, ro_recv.at[o, n]).start()

    def c_relay(n):
        @pl.when(x_lo == 0)
        def _():
            for t in (KEY, VALUE):
                take(c_in.at[t, n], ci_recv.at[t, n])
                send(c_in.at[t, n], c_low.at[t, n], cl_send.at[t, n], cl_recv.at[t, n], lo_peer)

    def r_relay(n):
        @pl.when(x_hi == 0)
        def _():
            for t in (KEY, VALUE):
                take(r_in.at[t, r_span(n)], ri_recv.at[t, n])
                send(
                    r_in.at[t, r_span(n)], r_low.at[t, r_span(n)],
                    rl_send.at[t, n], rl_recv.at[t, n], hi_peer,
                )

    def spread(slot, ref):
        f_in[slot] = ref[...].astype(F32).reshape(col_len * col_step, HEAD_DIM)

    def packed(n, slot):
        return f_out[n, slot].reshape(col_len, col_step, HEAD_DIM)

    def c_work(n):
        def column(slot, c):
            return f_in[slot, pl.ds(c, col_len, stride=col_step), :].astype(BF16)

        def put(slot, c, value):
            f_out[n, slot, pl.ds(c, col_len, stride=col_step), :] = value

        @pl.when(x_lo == 0)
        def _():
            for t in (QUERY, GRAD):
                take(c_in.at[t, n], ci_recv.at[t, n])
            for t in range(4):
                spread(t, c_in.at[t, n])

            def item(c, carry):
                parts = attend_back(
                    column(KEY, c), column(VALUE, c), column(QUERY, c), column(GRAD, c), 0
                )
                for o in range(3):
                    put(o, c, parts[o])
                return carry

            lax.fori_loop(0, col_step, item, 0, unroll=2)
            c_out[DQUERY, n] = packed(n, DQUERY).astype(BF16)
            c_send_out(DQUERY, n)

        @pl.when(x_lo == 1)
        def _():
            for t in range(4):
                take(c_in.at[t, n], ci_recv.at[t, n])
                spread(t, c_in.at[t, n])
            for t in (KEY, VALUE):
                take(c_low.at[t, n], cl_recv.at[t, n])
                spread(4 + t, c_low.at[t, n])

            def item(c, carry):
                keys = jnp.concatenate([column(4 + KEY, c), column(KEY, c)], axis=0)
                values = jnp.concatenate([column(4 + VALUE, c), column(VALUE, c)], axis=0)
                parts = attend_back(keys, values, column(QUERY, c), column(GRAD, c), col_len)
                put(DQUERY, c, parts[DQUERY])
                for o in (DKEY, DVALUE):
                    put(o, c, parts[o][col_len:])
                    put(3 + o, c, parts[o][:col_len])
                return carry

            lax.fori_loop(0, col_step, item, 0, unroll=2)
            for o in (DKEY, DVALUE):
                c_part[o, n] = packed(n, 3 + o).astype(BF16)
                send(c_part.at[o, n], c_back.at[o, n], cb_send.at[o, n], cb_recv.at[o, n], lo_peer)
            for o in (DQUERY, DKEY, DVALUE):
                c_out[o, n] = packed(n, o).astype(BF16)
                c_send_out(o, n)

    def c_finish(n):
        @pl.when(x_lo == 0)
        def _():
            for o in (DKEY, DVALUE):
                take(c_back.at[o, n], cb_recv.at[o, n])
                c_out[o, n] = (packed(n, o) + c_back[o, n].astype(F32)).astype(BF16)
                c_send_out(o, n)

    tile = row_len // 2

    def r_work(n):
        first = n * row_step

        @pl.when(x_hi == 0)
        def _():
            for t in (QUERY, GRAD):
                take(r_in.at[t, r_span(n)], ri_recv.at[t, n])

            def item(i, carry):
                at = first + i
                for o in (DKEY, DVALUE):
                    r_sum[o, at, tile:] = jnp.zeros((tile, HEAD_DIM), F32)
                for part in range(2):
                    seen = (part + 1) * tile
                    span = slice(part * tile, seen)
                    parts = attend_back(
                        r_in[KEY, at, :seen], r_in[VALUE, at, :seen],
                        r_in[QUERY, at, span], r_in[GRAD, at, span], part * tile,
                    )
                    for o in (DKEY, DVALUE):
                        if part == 0:
                            r_sum[o, at, :seen] = parts[o]
                        else:
                            r_sum[o, at, :seen] += parts[o]
                    r_out[DQUERY, at, span] = parts[DQUERY].astype(BF16)
                return carry

            lax.fori_loop(0, row_step, item, 0)
            r_send_out(DQUERY, n)

        @pl.when(x_hi == 1)
        def _():
            for t in range(4):
                take(r_in.at[t, r_span(n)], ri_recv.at[t, n])
            for t in (KEY, VALUE):
                take(r_low.at[t, r_span(n)], rl_recv.at[t, n])

            def item(i, carry):
                at = first + i
                sums = []
                for part in range(2):
                    seen = (part + 1) * tile
                    span = slice(part * tile, seen)
                    keys = jnp.concatenate([r_low[KEY, at], r_in[KEY, at, :seen]], axis=0)
                    values = jnp.concatenate([r_low[VALUE, at], r_in[VALUE, at, :seen]], axis=0)
                    parts = attend_back(
                        keys, values, r_in[QUERY, at, span], r_in[GRAD, at, span],
                        row_len + part * tile,
                    )
                    r_out[DQUERY, at, span] = parts[DQUERY].astype(BF16)
                    sums.append(parts)
                for o in (DKEY, DVALUE):
                    both = row_len + tile
                    total = sums[0][o] + sums[1][o][:both]
                    r_part[o, at] = total[:row_len].astype(BF16)
                    r_out[o, at, :tile] = total[row_len:].astype(BF16)
                    r_out[o, at, tile:] = sums[1][o][both:].astype(BF16)
                return carry

            lax.fori_loop(0, row_step, item, 0)
            for o in (DKEY, DVALUE):
                send(
                    r_part.at[o, r_span(n)], r_back.at[o, r_span(n)],
                    rb_send.at[o, n], rb_recv.at[o, n], hi_peer,
                )
            for o in (DQUERY, DKEY, DVALUE):
                r_send_out(o, n)

    def r_finish(n):
        @pl.when(x_hi == 0)
        def _():
            span = r_span(n)
            for o in (DKEY, DVALUE):
                take(r_back.at[o, span], rb_recv.at[o, n])
                r_out[o, span] = (r_sum[o, span] + r_back[o, span].astype(F32)).astype(BF16)
                r_send_out(o, n)

    for n in range(2):
        for t in (KEY, VALUE, QUERY, GRAD):
            c_send_in(t, n)
            r_send_in(t, n)

    r_relay(0)
    c_relay(0)
    r_work(0)
    r_relay(1)
    c_work(0)
    c_relay(1)
    r_work(1)
    r_finish(0)
    c_finish(0)
    c_work(1)
    r_finish(1)
    c_finish(1)

    sent = (RING - 1) * row_count
    sent_cols = (RING - 1) * col_count
    for n in range(2):
        for t in range(4):
            take(c_in.at[t, n, :sent], ci_send.at[t, n])
            take(r_in.at[t, r_span(n), :sent_cols], ri_send.at[t, n])
        for o in range(3):
            take(c_out.at[o, n, :sent], co_send.at[o, n])
            take(r_out.at[o, r_span(n), :sent_cols], ro_send.at[o, n])
            take(c_out.at[o, n], co_recv.at[o, n])
            take(r_out.at[o, r_span(n)], ro_recv.at[o, n])
        for t in (KEY, VALUE):
            @pl.when(x_lo == 0)
            def _():
                take(c_in.at[t, n], cl_send.at[t, n])

            @pl.when(x_lo == 1)
            def _():
                take(c_part.at[t, n], cb_send.at[t, n])

            @pl.when(x_hi == 0)
            def _():
                take(r_in.at[t, r_span(n)], rl_send.at[t, n])

            @pl.when(x_hi == 1)
            def _():
                take(r_part.at[t, r_span(n)], rb_send.at[t, n])


def body(queries, key_vectors, value_vectors, grad_output):
    row_count, col_count, width = queries.shape
    col_step = col_count // COL_CHUNKS
    col_len, row_len = row_count * RING, col_count * RING
    c_shape = (COL_CHUNKS, col_len, col_step, HEAD_DIM)
    r_shape = (row_count, row_len, HEAD_DIM)
    flat = (col_len * col_step, HEAD_DIM)
    dma = pltpu.SemaphoreType.DMA
    scratch = [
        pltpu.VMEM((4, *c_shape), BF16),
        pltpu.VMEM((2, *c_shape), BF16),
        pltpu.VMEM((3, *c_shape), BF16),
        pltpu.VMEM((2, *c_shape), BF16),
        pltpu.VMEM((2, *c_shape), BF16),
        pltpu.VMEM((6, *flat), F32),
        pltpu.VMEM((COL_CHUNKS, 5, *flat), F32),
        pltpu.VMEM((4, *r_shape), BF16),
        pltpu.VMEM((2, *r_shape), BF16),
        pltpu.VMEM((3, *r_shape), BF16),
        pltpu.VMEM((2, *r_shape), BF16),
        pltpu.VMEM((2, *r_shape), BF16),
        pltpu.VMEM((2, *r_shape), F32),
    ]
    for chunks in (COL_CHUNKS, ROW_CHUNKS):
        for arrays in (4, 2, 2, 3):
            scratch += [dma((arrays, chunks)), dma((arrays, chunks))]
    shape = jax.ShapeDtypeStruct(queries.shape, BF16)
    return pl.pallas_call(
        kernel,
        out_shape=(shape, shape, shape),
        in_specs=[pl.BlockSpec(memory_space=pl.ANY)] * 4,
        out_specs=[pl.BlockSpec(memory_space=pl.ANY)] * 3,
        scratch_shapes=scratch,
        compiler_params=pltpu.CompilerParams(
            collective_id=0, has_side_effects=True, vmem_limit_bytes=56 * 2**20
        ),
    )(queries, key_vectors, value_vectors, grad_output)


def solution(mesh):
    placed = P("row", "col", None)
    return jax.shard_map(
        body,
        mesh=mesh,
        in_specs=(placed,) * 4,
        out_specs=(placed,) * 3,
        check_vma=False,
    )
```

```python
import functools
import math

import jax
import jax.numpy as jnp
from jax import lax
from jax.experimental import pallas as pl
from jax.experimental.pallas import tpu as pltpu
from jax.sharding import PartitionSpec as P

MESH = pl.DeviceIdType.MESH
HEAD_DIM = 128
RING = 8
FACTOR = 1.0 / math.sqrt(HEAD_DIM)
LOG2E = math.log2(math.e)
BF16, F32 = jnp.bfloat16, jnp.float32

KEY, VALUE, QUERY, GRAD = range(4)
DKEY, DVALUE, DQUERY = range(3)
COL_CHUNKS = 2
ROW_CHUNKS = 2


def attend_back(keys, values, queries, grads, causal_from):
    key_count, query_count = keys.shape[0], queries.shape[0]
    contract_last = (((1,), (1,)), ((), ()))
    raw = lax.dot_general(keys, queries, contract_last, preferred_element_type=F32)
    key_at = lax.broadcasted_iota(jnp.int32, (key_count, query_count), 0)
    query_at = lax.broadcasted_iota(jnp.int32, (key_count, query_count), 1)
    raw = jnp.where(key_at <= query_at + causal_from, raw, -jnp.inf)
    highest = jnp.max(raw, axis=0, keepdims=True)
    weights = jnp.exp2((raw - highest) * (FACTOR * LOG2E))
    probs = weights * (1.0 / jnp.sum(weights, axis=0, keepdims=True))
    probs_low = probs.astype(BF16)
    grad_weights = lax.dot_general(values, grads, contract_last, preferred_element_type=F32)
    correction = jnp.sum(probs_low.astype(F32) * grad_weights, axis=0, keepdims=True)
    grad_scores = (probs * (grad_weights - correction)).astype(BF16)
    grad_values = jnp.dot(probs_low, grads, preferred_element_type=F32)
    grad_keys = jnp.dot(grad_scores, queries, preferred_element_type=F32) * FACTOR
    grad_queries = (
        lax.dot_general(grad_scores, keys, (((0,), (0,)), ((), ())), preferred_element_type=F32)
        * FACTOR
    )
    return grad_keys, grad_values, grad_queries


def kernel(
    q_ref, k_ref, v_ref, g_ref, dq_ref, dk_ref, dv_ref,
    c_in, c_low, c_out, c_part, c_back, f_in, f_out,
    r_in, r_low, r_out, r_part, r_back, r_sum,
    ci_send, ci_recv, cl_send, cl_recv, cb_send, cb_recv, co_send, co_recv,
    ri_send, ri_recv, rl_send, rl_recv, rb_send, rb_recv, ro_send, ro_recv,
):
    inputs = (k_ref, v_ref, q_ref, g_ref)
    outputs = (dk_ref, dv_ref, dq_ref)
    row_count, col_count, width = q_ref.shape
    half = width // 2
    col_step = col_count // COL_CHUNKS
    row_step = row_count // ROW_CHUNKS
    col_len = row_count * RING
    row_len = col_count * RING

    row = lax.axis_index("row")
    col = lax.axis_index("col")
    x_lo, z = row // RING, lax.rem(row, RING)
    x_hi, j = col // RING, lax.rem(col, RING)

    def z_peer(at):
        return (x_lo * RING + at, col)

    def j_peer(at):
        return (row, x_hi * RING + at)

    lo_peer = ((1 - x_lo) * RING + z, col)
    hi_peer = (row, (1 - x_hi) * RING + j)

    def others(start, step):
        def at(d, carry):
            step(lax.rem(start + d, RING))
            return carry

        lax.fori_loop(1, RING, at, 0)

    barrier = pltpu.get_barrier_semaphore()

    def greet(target):
        pl.semaphore_signal(barrier, inc=1, device_id=target, device_id_type=MESH)

    others(z, lambda at: greet(z_peer(at)))
    others(j, lambda at: greet(j_peer(at)))
    greet(lo_peer)
    greet(hi_peer)
    pl.semaphore_wait(barrier, 2 * RING)

    def lanes(first):
        return pl.ds(pl.multiple_of(first, HEAD_DIM), HEAD_DIM)

    def send(src, dst, send_sem, recv_sem, target):
        pltpu.make_async_remote_copy(
            src_ref=src, dst_ref=dst, send_sem=send_sem, recv_sem=recv_sem,
            device_id=target, device_id_type=MESH,
        ).start()

    def take(ref, sem):
        pltpu.make_async_copy(ref, ref, sem).wait()

    def c_rows(at):
        return pl.ds(at * row_count, row_count)

    def r_cols(at):
        return pl.ds(pl.multiple_of(at * col_count, col_count), col_count)

    def c_send_in(t, n):
        def src(at):
            return inputs[t].at[:, pl.ds(n * col_step, col_step), lanes(half + at * HEAD_DIM)]

        dst = c_in.at[t, n, c_rows(z)]
        others(z, lambda at: send(src(at), dst, ci_send.at[t, n], ci_recv.at[t, n], z_peer(at)))
        pltpu.make_async_copy(src(z), dst, ci_recv.at[t, n]).start()

    def c_send_out(o, n):
        dst = outputs[o].at[:, pl.ds(n * col_step, col_step), lanes(half + z * HEAD_DIM)]

        def src(at):
            return c_out.at[o, n, c_rows(at)]

        others(z, lambda at: send(src(at), dst, co_send.at[o, n], co_recv.at[o, n], z_peer(at)))
        pltpu.make_async_copy(src(z), dst, co_recv.at[o, n]).start()

    def r_span(n):
        return pl.ds(n * row_step, row_step)

    def r_send_in(t, n):
        def src(at):
            return inputs[t].at[r_span(n), :, lanes(at * HEAD_DIM)]

        dst = r_in.at[t, r_span(n), r_cols(j)]
        others(j, lambda at: send(src(at), dst, ri_send.at[t, n], ri_recv.at[t, n], j_peer(at)))
        pltpu.make_async_copy(src(j), dst, ri_recv.at[t, n]).start()

    def r_send_out(o, n):
        dst = outputs[o].at[r_span(n), :, lanes(j * HEAD_DIM)]

        def src(at):
            return r_out.at[o, r_span(n), r_cols(at)]

        others(j, lambda at: send(src(at), dst, ro_send.at[o, n], ro_recv.at[o, n], j_peer(at)))
        pltpu.make_async_copy(src(j), dst, ro_recv.at[o, n]).start()

    def c_relay(n):
        @pl.when(x_lo == 0)
        def _():
            for t in (KEY, VALUE):
                take(c_in.at[t, n], ci_recv.at[t, n])
                send(c_in.at[t, n], c_low.at[t, n], cl_send.at[t, n], cl_recv.at[t, n], lo_peer)

    def r_relay(n):
        @pl.when(x_hi == 0)
        def _():
            for t in (KEY, VALUE):
                take(r_in.at[t, r_span(n)], ri_recv.at[t, n])
                send(
                    r_in.at[t, r_span(n)], r_low.at[t, r_span(n)],
                    rl_send.at[t, n], rl_recv.at[t, n], hi_peer,
                )

    def spread(slot, ref):
        f_in[slot] = ref[...].astype(F32).reshape(col_len * col_step, HEAD_DIM)

    def packed(n, slot):
        return f_out[n, slot].reshape(col_len, col_step, HEAD_DIM)

    def c_work(n):
        def column(slot, c):
            return f_in[slot, pl.ds(c, col_len, stride=col_step), :].astype(BF16)

        def put(slot, c, value):
            f_out[n, slot, pl.ds(c, col_len, stride=col_step), :] = value

        @pl.when(x_lo == 0)
        def _():
            for t in (QUERY, GRAD):
                take(c_in.at[t, n], ci_recv.at[t, n])
            for t in range(4):
                spread(t, c_in.at[t, n])

            def item(c, carry):
                parts = attend_back(
                    column(KEY, c), column(VALUE, c), column(QUERY, c), column(GRAD, c), 0
                )
                for o in range(3):
                    put(o, c, parts[o])
                return carry

            lax.fori_loop(0, col_step, item, 0, unroll=2)
            c_out[DQUERY, n] = packed(n, DQUERY).astype(BF16)
            c_send_out(DQUERY, n)

        @pl.when(x_lo == 1)
        def _():
            for t in range(4):
                take(c_in.at[t, n], ci_recv.at[t, n])
                spread(t, c_in.at[t, n])
            for t in (KEY, VALUE):
                take(c_low.at[t, n], cl_recv.at[t, n])
                spread(4 + t, c_low.at[t, n])

            def item(c, carry):
                keys = jnp.concatenate([column(4 + KEY, c), column(KEY, c)], axis=0)
                values = jnp.concatenate([column(4 + VALUE, c), column(VALUE, c)], axis=0)
                parts = attend_back(keys, values, column(QUERY, c), column(GRAD, c), col_len)
                put(DQUERY, c, parts[DQUERY])
                for o in (DKEY, DVALUE):
                    put(o, c, parts[o][col_len:])
                    put(3 + o, c, parts[o][:col_len])
                return carry

            lax.fori_loop(0, col_step, item, 0, unroll=2)
            for o in (DKEY, DVALUE):
                c_part[o, n] = packed(n, 3 + o).astype(BF16)
                send(c_part.at[o, n], c_back.at[o, n], cb_send.at[o, n], cb_recv.at[o, n], lo_peer)
            for o in (DQUERY, DKEY, DVALUE):
                c_out[o, n] = packed(n, o).astype(BF16)
                c_send_out(o, n)

    def c_finish(n):
        @pl.when(x_lo == 0)
        def _():
            for o in (DKEY, DVALUE):
                take(c_back.at[o, n], cb_recv.at[o, n])
                c_out[o, n] = (packed(n, o) + c_back[o, n].astype(F32)).astype(BF16)
                c_send_out(o, n)

    tile = row_len // 2

    def r_work(n):
        first = n * row_step

        @pl.when(x_hi == 0)
        def _():
            for t in (QUERY, GRAD):
                take(r_in.at[t, r_span(n)], ri_recv.at[t, n])

            def item(i, carry):
                at = first + i
                for o in (DKEY, DVALUE):
                    r_sum[o, at, tile:] = jnp.zeros((tile, HEAD_DIM), F32)
                for part in range(2):
                    seen = (part + 1) * tile
                    span = slice(part * tile, seen)
                    parts = attend_back(
                        r_in[KEY, at, :seen], r_in[VALUE, at, :seen],
                        r_in[QUERY, at, span], r_in[GRAD, at, span], part * tile,
                    )
                    for o in (DKEY, DVALUE):
                        if part == 0:
                            r_sum[o, at, :seen] = parts[o]
                        else:
                            r_sum[o, at, :seen] += parts[o]
                    r_out[DQUERY, at, span] = parts[DQUERY].astype(BF16)
                return carry

            lax.fori_loop(0, row_step, item, 0)
            r_send_out(DQUERY, n)

        @pl.when(x_hi == 1)
        def _():
            for t in range(4):
                take(r_in.at[t, r_span(n)], ri_recv.at[t, n])
            for t in (KEY, VALUE):
                take(r_low.at[t, r_span(n)], rl_recv.at[t, n])

            def item(i, carry):
                at = first + i
                sums = []
                for part in range(2):
                    seen = (part + 1) * tile
                    span = slice(part * tile, seen)
                    keys = jnp.concatenate([r_low[KEY, at], r_in[KEY, at, :seen]], axis=0)
                    values = jnp.concatenate([r_low[VALUE, at], r_in[VALUE, at, :seen]], axis=0)
                    parts = attend_back(
                        keys, values, r_in[QUERY, at, span], r_in[GRAD, at, span],
                        row_len + part * tile,
                    )
                    r_out[DQUERY, at, span] = parts[DQUERY].astype(BF16)
                    sums.append(parts)
                for o in (DKEY, DVALUE):
                    both = row_len + tile
                    total = sums[0][o] + sums[1][o][:both]
                    r_part[o, at] = total[:row_len].astype(BF16)
                    r_out[o, at, :tile] = total[row_len:].astype(BF16)
                    r_out[o, at, tile:] = sums[1][o][both:].astype(BF16)
                return carry

            lax.fori_loop(0, row_step, item, 0)
            for o in (DKEY, DVALUE):
                send(
                    r_part.at[o, r_span(n)], r_back.at[o, r_span(n)],
                    rb_send.at[o, n], rb_recv.at[o, n], hi_peer,
                )
            for o in (DQUERY, DKEY, DVALUE):
                r_send_out(o, n)

    def r_finish(n):
        @pl.when(x_hi == 0)
        def _():
            span = r_span(n)
            for o in (DKEY, DVALUE):
                take(r_back.at[o, span], rb_recv.at[o, n])
                r_out[o, span] = (r_sum[o, span] + r_back[o, span].astype(F32)).astype(BF16)
                r_send_out(o, n)

    for n in range(2):
        for t in (KEY, VALUE, QUERY, GRAD):
            c_send_in(t, n)
            r_send_in(t, n)

    r_relay(0)
    c_relay(0)
    r_work(0)
    r_relay(1)
    c_work(0)
    c_relay(1)
    r_work(1)
    r_finish(0)
    c_finish(0)
    c_work(1)
    r_finish(1)
    c_finish(1)

    sent = (RING - 1) * row_count
    sent_cols = (RING - 1) * col_count
    for n in range(2):
        for t in range(4):
            take(c_in.at[t, n, :sent], ci_send.at[t, n])
            take(r_in.at[t, r_span(n), :sent_cols], ri_send.at[t, n])
        for o in range(3):
            take(c_out.at[o, n, :sent], co_send.at[o, n])
            take(r_out.at[o, r_span(n), :sent_cols], ro_send.at[o, n])
            take(c_out.at[o, n], co_recv.at[o, n])
            take(r_out.at[o, r_span(n)], ro_recv.at[o, n])
        for t in (KEY, VALUE):
            @pl.when(x_lo == 0)
            def _():
                take(c_in.at[t, n], cl_send.at[t, n])

            @pl.when(x_lo == 1)
            def _():
                take(c_part.at[t, n], cb_send.at[t, n])

            @pl.when(x_hi == 0)
            def _():
                take(r_in.at[t, r_span(n)], rl_send.at[t, n])

            @pl.when(x_hi == 1)
            def _():
                take(r_part.at[t, r_span(n)], rb_send.at[t, n])


def hand_out(*refs):
    sems = refs[-1]
    copies = [pltpu.make_async_copy(refs[o], refs[3 + o], sems.at[o]) for o in range(3)]
    for copy in copies:
        copy.start()
    for copy in copies:
        copy.wait()


def body(queries, key_vectors, value_vectors, grad_output):
    row_count, col_count, width = queries.shape
    col_step = col_count // COL_CHUNKS
    col_len, row_len = row_count * RING, col_count * RING
    c_shape = (COL_CHUNKS, col_len, col_step, HEAD_DIM)
    r_shape = (row_count, row_len, HEAD_DIM)
    flat = (col_len * col_step, HEAD_DIM)
    dma = pltpu.SemaphoreType.DMA
    scratch = [
        pltpu.VMEM((4, *c_shape), BF16),
        pltpu.VMEM((2, *c_shape), BF16),
        pltpu.VMEM((3, *c_shape), BF16),
        pltpu.VMEM((2, *c_shape), BF16),
        pltpu.VMEM((2, *c_shape), BF16),
        pltpu.VMEM((6, *flat), F32),
        pltpu.VMEM((COL_CHUNKS, 5, *flat), F32),
        pltpu.VMEM((4, *r_shape), BF16),
        pltpu.VMEM((2, *r_shape), BF16),
        pltpu.VMEM((3, *r_shape), BF16),
        pltpu.VMEM((2, *r_shape), BF16),
        pltpu.VMEM((2, *r_shape), BF16),
        pltpu.VMEM((2, *r_shape), F32),
    ]
    for chunks in (COL_CHUNKS, ROW_CHUNKS):
        for arrays in (4, 2, 2, 3):
            scratch += [dma((arrays, chunks)), dma((arrays, chunks))]
    shape = jax.ShapeDtypeStruct(queries.shape, BF16)
    grads = pl.pallas_call(
        kernel,
        out_shape=(shape, shape, shape),
        in_specs=[pl.BlockSpec(memory_space=pltpu.HBM)] * 4,
        out_specs=[pl.BlockSpec(memory_space=pl.ANY)] * 3,
        scratch_shapes=scratch,
        compiler_params=pltpu.CompilerParams(
            collective_id=0, has_side_effects=True, vmem_limit_bytes=48 * 2**20
        ),
    )(queries, key_vectors, value_vectors, grad_output)
    return pl.pallas_call(
        hand_out,
        out_shape=(shape, shape, shape),
        in_specs=[pl.BlockSpec(memory_space=pl.ANY)] * 3,
        out_specs=[pl.BlockSpec(memory_space=pltpu.HBM)] * 3,
        scratch_shapes=[dma((3,))],
        compiler_params=pltpu.CompilerParams(vmem_limit_bytes=8 * 2**20),
    )(*grads)


def solution(mesh):
    placed = P("row", "col", None)
    return jax.shard_map(
        body,
        mesh=mesh,
        in_specs=(placed,) * 4,
        out_specs=(placed,) * 3,
        check_vma=False,
    )
```

```python
import functools
import math

import jax
import jax.numpy as jnp
from jax import lax
from jax.experimental import pallas as pl
from jax.experimental.pallas import tpu as pltpu
from jax.sharding import PartitionSpec as P

MESH = pl.DeviceIdType.MESH
HEAD_DIM = 128
RING = 8
FACTOR = 1.0 / math.sqrt(HEAD_DIM)
LOG2E = math.log2(math.e)
BF16, F32 = jnp.bfloat16, jnp.float32

KEY, VALUE, QUERY, GRAD = range(4)
DKEY, DVALUE, DQUERY = range(3)
COL_CHUNKS = 2
ROW_CHUNKS = 2


def attend_back(keys, values, queries, grads, causal_from):
    key_count, query_count = keys.shape[0], queries.shape[0]
    contract_last = (((1,), (1,)), ((), ()))
    raw = lax.dot_general(keys, queries, contract_last, preferred_element_type=F32)
    key_at = lax.broadcasted_iota(jnp.int32, (key_count, query_count), 0)
    query_at = lax.broadcasted_iota(jnp.int32, (key_count, query_count), 1)
    raw = jnp.where(key_at <= query_at + causal_from, raw, -jnp.inf)
    highest = jnp.max(raw, axis=0, keepdims=True)
    weights = jnp.exp2((raw - highest) * (FACTOR * LOG2E))
    probs = weights * (1.0 / jnp.sum(weights, axis=0, keepdims=True))
    probs_low = probs.astype(BF16)
    grad_weights = lax.dot_general(values, grads, contract_last, preferred_element_type=F32)
    correction = jnp.sum(probs_low.astype(F32) * grad_weights, axis=0, keepdims=True)
    grad_scores = (probs * (grad_weights - correction)).astype(BF16)
    grad_values = jnp.dot(probs_low, grads, preferred_element_type=F32)
    grad_keys = jnp.dot(grad_scores, queries, preferred_element_type=F32) * FACTOR
    grad_queries = (
        lax.dot_general(grad_scores, keys, (((0,), (0,)), ((), ())), preferred_element_type=F32)
        * FACTOR
    )
    return grad_keys, grad_values, grad_queries


def kernel(
    q_ref, k_ref, v_ref, g_ref, dq_ref, dk_ref, dv_ref,
    c_in, c_low, c_out, c_part, c_back, f_in, f_out,
    r_in, r_low, r_out, r_part, r_back, r_sum,
    ci_send, ci_recv, cl_send, cl_recv, cb_send, cb_recv, co_send, co_recv,
    ri_send, ri_recv, rl_send, rl_recv, rb_send, rb_recv, ro_send, ro_recv, ring_sem, go_sem,
):
    inputs = (k_ref, v_ref, q_ref, g_ref)
    outputs = (dk_ref, dv_ref, dq_ref)
    row_count, col_count, width = q_ref.shape
    half = width // 2
    col_step = col_count // COL_CHUNKS
    row_step = row_count // ROW_CHUNKS
    col_len = row_count * RING
    row_len = col_count * RING

    row = lax.axis_index("row")
    col = lax.axis_index("col")
    x_lo, z = row // RING, lax.rem(row, RING)
    x_hi, j = col // RING, lax.rem(col, RING)

    def z_peer(at):
        return (x_lo * RING + at, col)

    def j_peer(at):
        return (row, x_hi * RING + at)

    lo_peer = ((1 - x_lo) * RING + z, col)
    hi_peer = (row, (1 - x_hi) * RING + j)

    def others(start, step):
        def at(d, carry):
            step(lax.rem(start + d, RING))
            return carry

        lax.fori_loop(1, RING, at, 0)

    barrier = pltpu.get_barrier_semaphore()

    def signal(sem, target):
        pl.semaphore_signal(sem, inc=1, device_id=target, device_id_type=MESH)

    def signal_rings(sem):
        others(j, lambda at: signal(sem, j_peer(at)))
        signal(sem, lo_peer)
        signal(sem, hi_peer)

    others(z, lambda at: signal(barrier, z_peer(at)))

    @pl.when(z == 0)
    def _():
        signal_rings(barrier)
        pl.semaphore_wait(barrier, RING - 1 + RING + 1)

    @pl.when(z != 0)
    def _():
        pl.semaphore_wait(barrier, RING - 1)

    def lanes(first):
        return pl.ds(pl.multiple_of(first, HEAD_DIM), HEAD_DIM)

    def send(src, dst, send_sem, recv_sem, target):
        pltpu.make_async_remote_copy(
            src_ref=src, dst_ref=dst, send_sem=send_sem, recv_sem=recv_sem,
            device_id=target, device_id_type=MESH,
        ).start()

    def take(ref, sem):
        pltpu.make_async_copy(ref, ref, sem).wait()

    def c_rows(at):
        return pl.ds(at * row_count, row_count)

    def r_cols(at):
        return pl.ds(pl.multiple_of(at * col_count, col_count), col_count)

    def c_send_in(t, n):
        def src(at):
            return inputs[t].at[:, pl.ds(n * col_step, col_step), lanes(half + at * HEAD_DIM)]

        dst = c_in.at[t, n, c_rows(z)]
        others(z, lambda at: send(src(at), dst, ci_send.at[t, n], ci_recv.at[t, n], z_peer(at)))
        pltpu.make_async_copy(src(z), dst, ci_recv.at[t, n]).start()

    def c_send_out(tensors, n, order):
        def one(o, at):
            src = c_out.at[o, n, c_rows(at)]
            dst = outputs[o].at[:, pl.ds(n * col_step, col_step), lanes(half + z * HEAD_DIM)]

            @pl.when(at != z)
            def _():
                send(src, dst, co_send.at[o, n], co_recv.at[o, n], z_peer(at))

            @pl.when(at == z)
            def _():
                pltpu.make_async_copy(src, dst, co_recv.at[o, n]).start()

        def step(i, carry):
            for o in tensors:
                one(o, order(i))
            return carry

        lax.fori_loop(0, RING, step, 0)

    def round_from_here(i):
        return lax.rem(z + i, RING)

    def early_first(i):
        later = RING // 2 + lax.rem(z + i // 2, RING // 2)
        return jnp.where(lax.rem(i, 2) == 0, i // 2, later)

    def r_span(n):
        return pl.ds(n * row_step, row_step)

    def r_send_in(t, n):
        def src(at):
            return inputs[t].at[r_span(n), :, lanes(at * HEAD_DIM)]

        dst = r_in.at[t, r_span(n), r_cols(j)]
        others(j, lambda at: send(src(at), dst, ri_send.at[t, n], ri_recv.at[t, n], j_peer(at)))
        pltpu.make_async_copy(src(j), dst, ri_recv.at[t, n]).start()

    def r_send_out(o, n):
        dst = outputs[o].at[r_span(n), :, lanes(j * HEAD_DIM)]

        def src(at):
            return r_out.at[o, r_span(n), r_cols(at)]

        others(j, lambda at: send(src(at), dst, ro_send.at[o, n], ro_recv.at[o, n], j_peer(at)))
        pltpu.make_async_copy(src(j), dst, ro_recv.at[o, n]).start()

    def c_relay(n):
        @pl.when(x_lo == 0)
        def _():
            for t in (KEY, VALUE):
                take(c_in.at[t, n], ci_recv.at[t, n])
                send(c_in.at[t, n], c_low.at[t, n], cl_send.at[t, n], cl_recv.at[t, n], lo_peer)

    def r_relay(n):
        @pl.when(x_hi == 0)
        def _():
            for t in (KEY, VALUE):
                take(r_in.at[t, r_span(n)], ri_recv.at[t, n])
                send(
                    r_in.at[t, r_span(n)], r_low.at[t, r_span(n)],
                    rl_send.at[t, n], rl_recv.at[t, n], hi_peer,
                )

    def spread(slot, ref):
        f_in[slot] = ref[...].astype(F32).reshape(col_len * col_step, HEAD_DIM)

    def packed(n, slot):
        return f_out[n, slot].reshape(col_len, col_step, HEAD_DIM)

    def c_work(n):
        def column(slot, c):
            return f_in[slot, pl.ds(c, col_len, stride=col_step), :].astype(BF16)

        def put(slot, c, value):
            f_out[n, slot, pl.ds(c, col_len, stride=col_step), :] = value

        @pl.when(x_lo == 0)
        def _():
            for t in (KEY, VALUE):
                spread(t, c_in.at[t, n])
            for t in (QUERY, GRAD):
                take(c_in.at[t, n], ci_recv.at[t, n])
                spread(t, c_in.at[t, n])

            def item(c, carry):
                parts = attend_back(
                    column(KEY, c), column(VALUE, c), column(QUERY, c), column(GRAD, c), 0
                )
                for o in range(3):
                    put(o, c, parts[o])
                return carry

            lax.fori_loop(0, col_step, item, 0, unroll=4)
            c_out[DQUERY, n] = packed(n, DQUERY).astype(BF16)
            c_send_out((DQUERY,), n, round_from_here)

        @pl.when(x_lo == 1)
        def _():
            for t in (KEY, VALUE):
                take(c_in.at[t, n], ci_recv.at[t, n])
                spread(t, c_in.at[t, n])
                take(c_low.at[t, n], cl_recv.at[t, n])
                spread(4 + t, c_low.at[t, n])
            for t in (QUERY, GRAD):
                take(c_in.at[t, n], ci_recv.at[t, n])
                spread(t, c_in.at[t, n])

            def item(c, carry):
                keys = jnp.concatenate([column(4 + KEY, c), column(KEY, c)], axis=0)
                values = jnp.concatenate([column(4 + VALUE, c), column(VALUE, c)], axis=0)
                parts = attend_back(keys, values, column(QUERY, c), column(GRAD, c), col_len)
                put(DQUERY, c, parts[DQUERY])
                for o in (DKEY, DVALUE):
                    put(o, c, parts[o][col_len:])
                    put(3 + o, c, parts[o][:col_len])
                return carry

            lax.fori_loop(0, col_step, item, 0, unroll=4)
            for o in (DKEY, DVALUE):
                c_part[o, n] = packed(n, 3 + o).astype(BF16)
                send(c_part.at[o, n], c_back.at[o, n], cb_send.at[o, n], cb_recv.at[o, n], lo_peer)
            for o in (DQUERY, DKEY, DVALUE):
                c_out[o, n] = packed(n, o).astype(BF16)
                last = n == 1 and o == DVALUE
                c_send_out((o,), n, early_first if last else round_from_here)

    def c_finish(n):
        @pl.when(x_lo == 0)
        def _():
            for o in (DKEY, DVALUE):
                take(c_back.at[o, n], cb_recv.at[o, n])
                c_out[o, n] = (packed(n, o) + c_back[o, n].astype(F32)).astype(BF16)
                last = n == 1 and o == DVALUE
                c_send_out((o,), n, early_first if last else round_from_here)

    tile = row_len // 2

    def r_work(n):
        first = n * row_step

        @pl.when(x_hi == 0)
        def _():
            for t in (QUERY, GRAD):
                take(r_in.at[t, r_span(n)], ri_recv.at[t, n])

            def item(i, carry):
                at = first + i
                for o in (DKEY, DVALUE):
                    r_sum[o, at, tile:] = jnp.zeros((tile, HEAD_DIM), F32)
                for part in range(2):
                    seen = (part + 1) * tile
                    span = slice(part * tile, seen)
                    parts = attend_back(
                        r_in[KEY, at, :seen], r_in[VALUE, at, :seen],
                        r_in[QUERY, at, span], r_in[GRAD, at, span], part * tile,
                    )
                    for o in (DKEY, DVALUE):
                        if part == 0:
                            r_sum[o, at, :seen] = parts[o]
                        else:
                            r_sum[o, at, :seen] += parts[o]
                    r_out[DQUERY, at, span] = parts[DQUERY].astype(BF16)
                return carry

            lax.fori_loop(0, row_step, item, 0)
            r_send_out(DQUERY, n)

        @pl.when(x_hi == 1)
        def _():
            for t in range(4):
                take(r_in.at[t, r_span(n)], ri_recv.at[t, n])
            for t in (KEY, VALUE):
                take(r_low.at[t, r_span(n)], rl_recv.at[t, n])

            def item(i, carry):
                at = first + i
                sums = []
                for part in range(2):
                    seen = (part + 1) * tile
                    span = slice(part * tile, seen)
                    keys = jnp.concatenate([r_low[KEY, at], r_in[KEY, at, :seen]], axis=0)
                    values = jnp.concatenate([r_low[VALUE, at], r_in[VALUE, at, :seen]], axis=0)
                    parts = attend_back(
                        keys, values, r_in[QUERY, at, span], r_in[GRAD, at, span],
                        row_len + part * tile,
                    )
                    r_out[DQUERY, at, span] = parts[DQUERY].astype(BF16)
                    sums.append(parts)
                for o in (DKEY, DVALUE):
                    both = row_len + tile
                    total = sums[0][o] + sums[1][o][:both]
                    r_part[o, at] = total[:row_len].astype(BF16)
                    r_out[o, at, :tile] = total[row_len:].astype(BF16)
                    r_out[o, at, tile:] = sums[1][o][both:].astype(BF16)
                return carry

            lax.fori_loop(0, row_step, item, 0)
            for o in (DKEY, DVALUE):
                send(
                    r_part.at[o, r_span(n)], r_back.at[o, r_span(n)],
                    rb_send.at[o, n], rb_recv.at[o, n], hi_peer,
                )
            for o in (DQUERY, DKEY, DVALUE):
                r_send_out(o, n)

    def r_finish(n):
        @pl.when(x_hi == 0)
        def _():
            span = r_span(n)
            for o in (DKEY, DVALUE):
                take(r_back.at[o, span], rb_recv.at[o, n])
                r_out[o, span] = (r_sum[o, span] + r_back[o, span].astype(F32)).astype(BF16)
                r_send_out(o, n)

    for n in range(COL_CHUNKS):
        for t in (KEY, VALUE, QUERY, GRAD):
            c_send_in(t, n)

    @pl.when(z == 0)
    def _():
        signal_rings(ring_sem)
        pl.semaphore_wait(ring_sem, RING + 1)
        others(z, lambda at: signal(go_sem, z_peer(at)))

    @pl.when(z != 0)
    def _():
        pl.semaphore_wait(go_sem, 1)

    for n in range(ROW_CHUNKS):
        for t in (KEY, VALUE, QUERY, GRAD):
            r_send_in(t, n)

    r_relay(0)
    c_relay(0)
    r_work(0)
    r_relay(1)
    c_work(0)
    c_relay(1)
    r_work(1)
    r_finish(0)
    c_finish(0)
    c_work(1)
    c_finish(1)
    r_finish(1)

    sent = (RING - 1) * row_count
    sent_cols = (RING - 1) * col_count
    for n in range(2):
        for t in range(4):
            take(c_in.at[t, n, :sent], ci_send.at[t, n])
            take(r_in.at[t, r_span(n), :sent_cols], ri_send.at[t, n])
        for t in (KEY, VALUE):
            @pl.when(x_lo == 0)
            def _():
                take(c_in.at[t, n], cl_send.at[t, n])

            @pl.when(x_lo == 1)
            def _():
                take(c_part.at[t, n], cb_send.at[t, n])

            @pl.when(x_hi == 0)
            def _():
                take(r_in.at[t, r_span(n)], rl_send.at[t, n])

            @pl.when(x_hi == 1)
            def _():
                take(r_part.at[t, r_span(n)], rb_send.at[t, n])
        for o in (DQUERY, DKEY, DVALUE):
            take(r_out.at[o, r_span(n), :sent_cols], ro_send.at[o, n])
            take(r_out.at[o, r_span(n)], ro_recv.at[o, n])
    for n in range(2):
        for o in (DQUERY, DKEY, DVALUE):
            take(c_out.at[o, n, :sent], co_send.at[o, n])
            take(c_out.at[o, n], co_recv.at[o, n])


def hand_out(*refs):
    sems = refs[-1]
    copies = [pltpu.make_async_copy(refs[o], refs[3 + o], sems.at[o]) for o in range(3)]
    for copy in copies:
        copy.start()
    for copy in copies:
        copy.wait()


def body(queries, key_vectors, value_vectors, grad_output):
    row_count, col_count, width = queries.shape
    col_step = col_count // COL_CHUNKS
    col_len, row_len = row_count * RING, col_count * RING
    c_shape = (COL_CHUNKS, col_len, col_step, HEAD_DIM)
    r_shape = (row_count, row_len, HEAD_DIM)
    flat = (col_len * col_step, HEAD_DIM)
    dma = pltpu.SemaphoreType.DMA
    scratch = [
        pltpu.VMEM((4, *c_shape), BF16),
        pltpu.VMEM((2, *c_shape), BF16),
        pltpu.VMEM((3, *c_shape), BF16),
        pltpu.VMEM((2, *c_shape), BF16),
        pltpu.VMEM((2, *c_shape), BF16),
        pltpu.VMEM((6, *flat), F32),
        pltpu.VMEM((COL_CHUNKS, 5, *flat), F32),
        pltpu.VMEM((4, *r_shape), BF16),
        pltpu.VMEM((2, *r_shape), BF16),
        pltpu.VMEM((3, *r_shape), BF16),
        pltpu.VMEM((2, *r_shape), BF16),
        pltpu.VMEM((2, *r_shape), BF16),
        pltpu.VMEM((2, *r_shape), F32),
    ]
    for chunks in (COL_CHUNKS, ROW_CHUNKS):
        for arrays in (4, 2, 2, 3):
            scratch += [dma((arrays, chunks)), dma((arrays, chunks))]
    scratch += [pltpu.SemaphoreType.REGULAR, pltpu.SemaphoreType.REGULAR]
    shape = jax.ShapeDtypeStruct(queries.shape, BF16)
    grads = pl.pallas_call(
        kernel,
        out_shape=(shape, shape, shape),
        in_specs=[pl.BlockSpec(memory_space=pltpu.HBM)] * 4,
        out_specs=[pl.BlockSpec(memory_space=pl.ANY)] * 3,
        scratch_shapes=scratch,
        compiler_params=pltpu.CompilerParams(
            collective_id=0, has_side_effects=True, vmem_limit_bytes=48 * 2**20
        ),
    )(queries, key_vectors, value_vectors, grad_output)
    return pl.pallas_call(
        hand_out,
        out_shape=(shape, shape, shape),
        in_specs=[pl.BlockSpec(memory_space=pl.ANY)] * 3,
        out_specs=[pl.BlockSpec(memory_space=pltpu.HBM)] * 3,
        scratch_shapes=[dma((3,))],
        compiler_params=pltpu.CompilerParams(vmem_limit_bytes=8 * 2**20),
    )(*grads)


def solution(mesh):
    placed = P("row", "col", None)
    return jax.shard_map(
        body,
        mesh=mesh,
        in_specs=(placed,) * 4,
        out_specs=(placed,) * 3,
        check_vma=False,
    )
```

```python
import functools
import math

import jax
import jax.numpy as jnp
from jax import lax
from jax.experimental import pallas as pl
from jax.experimental.pallas import tpu as pltpu
from jax.sharding import PartitionSpec as P

MESH = pl.DeviceIdType.MESH
HEAD_DIM = 128
RING = 8
FACTOR = 1.0 / math.sqrt(HEAD_DIM)
LOG2E = math.log2(math.e)
BF16, F32 = jnp.bfloat16, jnp.float32

KEY, VALUE, QUERY, GRAD = range(4)
DKEY, DVALUE, DQUERY = range(3)
COL_CHUNKS = 2
ROW_CHUNKS = 2


def attend_back(keys, values, queries, grads, causal_from):
    key_count, query_count = keys.shape[0], queries.shape[0]
    contract_last = (((1,), (1,)), ((), ()))
    raw = lax.dot_general(keys, queries, contract_last, preferred_element_type=F32)
    key_at = lax.broadcasted_iota(jnp.int32, (key_count, query_count), 0)
    query_at = lax.broadcasted_iota(jnp.int32, (key_count, query_count), 1)
    raw = jnp.where(key_at <= query_at + causal_from, raw, -jnp.inf)
    highest = jnp.max(raw, axis=0, keepdims=True)
    weights = jnp.exp2((raw - highest) * (FACTOR * LOG2E))
    probs = weights * (1.0 / jnp.sum(weights, axis=0, keepdims=True))
    probs_low = probs.astype(BF16)
    grad_weights = lax.dot_general(values, grads, contract_last, preferred_element_type=F32)
    correction = jnp.sum(probs_low.astype(F32) * grad_weights, axis=0, keepdims=True)
    grad_scores = (probs * (grad_weights - correction)).astype(BF16)
    grad_values = jnp.dot(probs_low, grads, preferred_element_type=F32)
    grad_keys = jnp.dot(grad_scores, queries, preferred_element_type=F32) * FACTOR
    grad_queries = (
        lax.dot_general(grad_scores, keys, (((0,), (0,)), ((), ())), preferred_element_type=F32)
        * FACTOR
    )
    return grad_keys, grad_values, grad_queries


def kernel(
    q_ref, k_ref, v_ref, g_ref, dq_ref, dk_ref, dv_ref,
    c_in, c_low, c_out, c_part, c_back, f_in, f_out,
    r_in, r_low, r_out, r_part, r_back, r_sum,
    ci_send, ci_recv, cl_send, cl_recv, cb_send, cb_recv, co_send, co_recv,
    ri_send, ri_recv, rl_send, rl_recv, rb_send, rb_recv, ro_send, ro_recv, ring_sem, go_sem,
):
    inputs = (k_ref, v_ref, q_ref, g_ref)
    outputs = (dk_ref, dv_ref, dq_ref)
    row_count, col_count, width = q_ref.shape
    half = width // 2
    col_step = col_count // COL_CHUNKS
    row_step = row_count // ROW_CHUNKS
    col_len = row_count * RING
    row_len = col_count * RING

    row = lax.axis_index("row")
    col = lax.axis_index("col")
    x_lo, z = row // RING, lax.rem(row, RING)
    x_hi, j = col // RING, lax.rem(col, RING)

    def z_peer(at):
        return (x_lo * RING + at, col)

    def j_peer(at):
        return (row, x_hi * RING + at)

    lo_peer = ((1 - x_lo) * RING + z, col)
    hi_peer = (row, (1 - x_hi) * RING + j)

    def others(start, step):
        def at(d, carry):
            step(lax.rem(start + d, RING))
            return carry

        lax.fori_loop(1, RING, at, 0)

    barrier = pltpu.get_barrier_semaphore()

    def signal(sem, target):
        pl.semaphore_signal(sem, inc=1, device_id=target, device_id_type=MESH)

    def signal_rings(sem):
        others(j, lambda at: signal(sem, j_peer(at)))
        signal(sem, lo_peer)
        signal(sem, hi_peer)

    others(z, lambda at: signal(barrier, z_peer(at)))

    @pl.when(z == 0)
    def _():
        signal_rings(barrier)
        pl.semaphore_wait(barrier, RING - 1 + RING + 1)

    @pl.when(z != 0)
    def _():
        pl.semaphore_wait(barrier, RING - 1)

    def lanes(first):
        return pl.ds(pl.multiple_of(first, HEAD_DIM), HEAD_DIM)

    def send(src, dst, send_sem, recv_sem, target):
        pltpu.make_async_remote_copy(
            src_ref=src, dst_ref=dst, send_sem=send_sem, recv_sem=recv_sem,
            device_id=target, device_id_type=MESH,
        ).start()

    def take(ref, sem):
        pltpu.make_async_copy(ref, ref, sem).wait()

    def c_rows(at):
        return pl.ds(at * row_count, row_count)

    def r_cols(at):
        return pl.ds(pl.multiple_of(at * col_count, col_count), col_count)

    def c_send_in(t, n):
        def src(at):
            return inputs[t].at[:, pl.ds(n * col_step, col_step), lanes(half + at * HEAD_DIM)]

        dst = c_in.at[t, n, c_rows(z)]
        others(z, lambda at: send(src(at), dst, ci_send.at[t, n], ci_recv.at[t, n], z_peer(at)))
        pltpu.make_async_copy(src(z), dst, ci_recv.at[t, n]).start()

    def c_send_out(tensors, n, order):
        def one(o, at):
            src = c_out.at[o, n, c_rows(at)]
            dst = outputs[o].at[:, pl.ds(n * col_step, col_step), lanes(half + z * HEAD_DIM)]

            @pl.when(at != z)
            def _():
                send(src, dst, co_send.at[o, n], co_recv.at[o, n], z_peer(at))

            @pl.when(at == z)
            def _():
                pltpu.make_async_copy(src, dst, co_recv.at[o, n]).start()

        def step(i, carry):
            for o in tensors:
                one(o, order(i))
            return carry

        lax.fori_loop(0, RING, step, 0)

    def round_from_here(i):
        return lax.rem(z + i, RING)

    def early_first(i):
        later = RING // 2 + lax.rem(z + i // 2, RING // 2)
        return jnp.where(lax.rem(i, 2) == 0, i // 2, later)

    def r_span(n):
        return pl.ds(n * row_step, row_step)

    def r_send_in(t, n):
        def src(at):
            return inputs[t].at[r_span(n), :, lanes(at * HEAD_DIM)]

        dst = r_in.at[t, r_span(n), r_cols(j)]
        others(j, lambda at: send(src(at), dst, ri_send.at[t, n], ri_recv.at[t, n], j_peer(at)))
        pltpu.make_async_copy(src(j), dst, ri_recv.at[t, n]).start()

    def r_send_out(o, n):
        dst = outputs[o].at[r_span(n), :, lanes(j * HEAD_DIM)]

        def src(at):
            return r_out.at[o, r_span(n), r_cols(at)]

        others(j, lambda at: send(src(at), dst, ro_send.at[o, n], ro_recv.at[o, n], j_peer(at)))
        pltpu.make_async_copy(src(j), dst, ro_recv.at[o, n]).start()

    def c_relay(n):
        @pl.when(x_lo == 0)
        def _():
            for t in (KEY, VALUE):
                take(c_in.at[t, n], ci_recv.at[t, n])
                send(c_in.at[t, n], c_low.at[t, n], cl_send.at[t, n], cl_recv.at[t, n], lo_peer)

    def r_relay(n):
        @pl.when(x_hi == 0)
        def _():
            for t in (KEY, VALUE):
                take(r_in.at[t, r_span(n)], ri_recv.at[t, n])
                send(
                    r_in.at[t, r_span(n)], r_low.at[t, r_span(n)],
                    rl_send.at[t, n], rl_recv.at[t, n], hi_peer,
                )

    def spread(slot, ref):
        f_in[slot] = ref[...].astype(F32).reshape(col_len * col_step, HEAD_DIM)

    def packed(n, slot):
        return f_out[n, slot].reshape(col_len, col_step, HEAD_DIM)

    def c_work(n):
        def column(slot, c):
            return f_in[slot, pl.ds(c, col_len, stride=col_step), :].astype(BF16)

        def put(slot, c, value):
            f_out[n, slot, pl.ds(c, col_len, stride=col_step), :] = value

        @pl.when(x_lo == 0)
        def _():
            for t in (KEY, VALUE):
                spread(t, c_in.at[t, n])
            for t in (QUERY, GRAD):
                take(c_in.at[t, n], ci_recv.at[t, n])
                spread(t, c_in.at[t, n])

            def item(c, carry):
                parts = attend_back(
                    column(KEY, c), column(VALUE, c), column(QUERY, c), column(GRAD, c), 0
                )
                for o in range(3):
                    put(o, c, parts[o])
                return carry

            lax.fori_loop(0, col_step, item, 0, unroll=4)
            c_out[DQUERY, n] = packed(n, DQUERY).astype(BF16)
            c_send_out((DQUERY,), n, round_from_here)

        @pl.when(x_lo == 1)
        def _():
            for t in (KEY, VALUE):
                take(c_in.at[t, n], ci_recv.at[t, n])
                spread(t, c_in.at[t, n])
                take(c_low.at[t, n], cl_recv.at[t, n])
                spread(4 + t, c_low.at[t, n])
            for t in (QUERY, GRAD):
                take(c_in.at[t, n], ci_recv.at[t, n])
                spread(t, c_in.at[t, n])

            def item(c, carry):
                keys = jnp.concatenate([column(4 + KEY, c), column(KEY, c)], axis=0)
                values = jnp.concatenate([column(4 + VALUE, c), column(VALUE, c)], axis=0)
                parts = attend_back(keys, values, column(QUERY, c), column(GRAD, c), col_len)
                put(DQUERY, c, parts[DQUERY])
                for o in (DKEY, DVALUE):
                    put(o, c, parts[o][col_len:])
                    put(3 + o, c, parts[o][:col_len])
                return carry

            lax.fori_loop(0, col_step, item, 0, unroll=4)
            for o in (DKEY, DVALUE):
                c_part[o, n] = packed(n, 3 + o).astype(BF16)
                send(c_part.at[o, n], c_back.at[o, n], cb_send.at[o, n], cb_recv.at[o, n], lo_peer)
            for o in (DQUERY, DKEY, DVALUE):
                c_out[o, n] = packed(n, o).astype(BF16)
                last = n == 1 and o == DVALUE
                c_send_out((o,), n, early_first if last else round_from_here)

    def c_finish(n):
        @pl.when(x_lo == 0)
        def _():
            for o in (DKEY, DVALUE):
                take(c_back.at[o, n], cb_recv.at[o, n])
                c_out[o, n] = (packed(n, o) + c_back[o, n].astype(F32)).astype(BF16)
                last = n == 1 and o == DVALUE
                c_send_out((o,), n, early_first if last else round_from_here)

    tile = row_len // 2

    def r_work(n):
        first = n * row_step

        @pl.when(x_hi == 0)
        def _():
            for t in (QUERY, GRAD):
                take(r_in.at[t, r_span(n)], ri_recv.at[t, n])

            def item(i, carry):
                at = first + i
                for o in (DKEY, DVALUE):
                    r_sum[o, at, tile:] = jnp.zeros((tile, HEAD_DIM), F32)
                for part in range(2):
                    seen = (part + 1) * tile
                    span = slice(part * tile, seen)
                    parts = attend_back(
                        r_in[KEY, at, :seen], r_in[VALUE, at, :seen],
                        r_in[QUERY, at, span], r_in[GRAD, at, span], part * tile,
                    )
                    for o in (DKEY, DVALUE):
                        if part == 0:
                            r_sum[o, at, :seen] = parts[o]
                        else:
                            r_sum[o, at, :seen] += parts[o]
                    r_out[DQUERY, at, span] = parts[DQUERY].astype(BF16)
                return carry

            lax.fori_loop(0, row_step, item, 0)
            r_send_out(DQUERY, n)

        @pl.when(x_hi == 1)
        def _():
            for t in range(4):
                take(r_in.at[t, r_span(n)], ri_recv.at[t, n])
            for t in (KEY, VALUE):
                take(r_low.at[t, r_span(n)], rl_recv.at[t, n])

            def item(i, carry):
                at = first + i
                sums = []
                for part in range(2):
                    seen = (part + 1) * tile
                    span = slice(part * tile, seen)
                    keys = jnp.concatenate([r_low[KEY, at], r_in[KEY, at, :seen]], axis=0)
                    values = jnp.concatenate([r_low[VALUE, at], r_in[VALUE, at, :seen]], axis=0)
                    parts = attend_back(
                        keys, values, r_in[QUERY, at, span], r_in[GRAD, at, span],
                        row_len + part * tile,
                    )
                    r_out[DQUERY, at, span] = parts[DQUERY].astype(BF16)
                    sums.append(parts)
                for o in (DKEY, DVALUE):
                    both = row_len + tile
                    total = sums[0][o] + sums[1][o][:both]
                    r_part[o, at] = total[:row_len].astype(BF16)
                    r_out[o, at, :tile] = total[row_len:].astype(BF16)
                    r_out[o, at, tile:] = sums[1][o][both:].astype(BF16)
                return carry

            lax.fori_loop(0, row_step, item, 0)
            for o in (DKEY, DVALUE):
                send(
                    r_part.at[o, r_span(n)], r_back.at[o, r_span(n)],
                    rb_send.at[o, n], rb_recv.at[o, n], hi_peer,
                )
            for o in (DQUERY, DKEY, DVALUE):
                r_send_out(o, n)

    def r_finish(n):
        @pl.when(x_hi == 0)
        def _():
            span = r_span(n)
            for o in (DKEY, DVALUE):
                take(r_back.at[o, span], rb_recv.at[o, n])
                r_out[o, span] = (r_sum[o, span] + r_back[o, span].astype(F32)).astype(BF16)
                r_send_out(o, n)

    for n in range(COL_CHUNKS):
        for t in (KEY, VALUE, QUERY, GRAD):
            c_send_in(t, n)

    @pl.when(z == 0)
    def _():
        signal_rings(ring_sem)
        pl.semaphore_wait(ring_sem, RING + 1)
        others(z, lambda at: signal(go_sem, z_peer(at)))

    @pl.when(z != 0)
    def _():
        pl.semaphore_wait(go_sem, 1)

    for n in range(ROW_CHUNKS):
        for t in (KEY, VALUE, QUERY, GRAD):
            r_send_in(t, n)

    c_relay(0)
    r_relay(0)
    r_work(0)
    r_relay(1)
    c_work(0)
    c_relay(1)
    r_work(1)
    r_finish(0)
    c_finish(0)
    c_work(1)
    c_finish(1)
    r_finish(1)

    sent = (RING - 1) * row_count
    sent_cols = (RING - 1) * col_count
    for n in range(2):
        for t in range(4):
            take(c_in.at[t, n, :sent], ci_send.at[t, n])
            take(r_in.at[t, r_span(n), :sent_cols], ri_send.at[t, n])
        for t in (KEY, VALUE):
            @pl.when(x_lo == 0)
            def _():
                take(c_in.at[t, n], cl_send.at[t, n])

            @pl.when(x_lo == 1)
            def _():
                take(c_part.at[t, n], cb_send.at[t, n])

            @pl.when(x_hi == 0)
            def _():
                take(r_in.at[t, r_span(n)], rl_send.at[t, n])

            @pl.when(x_hi == 1)
            def _():
                take(r_part.at[t, r_span(n)], rb_send.at[t, n])
        for o in (DQUERY, DKEY, DVALUE):
            take(r_out.at[o, r_span(n), :sent_cols], ro_send.at[o, n])
            take(r_out.at[o, r_span(n)], ro_recv.at[o, n])
    for n in range(2):
        for o in (DQUERY, DKEY, DVALUE):
            take(c_out.at[o, n, :sent], co_send.at[o, n])
            take(c_out.at[o, n], co_recv.at[o, n])


def hand_out(*refs):
    sems = refs[-1]
    copies = [pltpu.make_async_copy(refs[o], refs[3 + o], sems.at[o]) for o in range(3)]
    for copy in copies:
        copy.start()
    for copy in copies:
        copy.wait()


def body(queries, key_vectors, value_vectors, grad_output):
    row_count, col_count, width = queries.shape
    col_step = col_count // COL_CHUNKS
    col_len, row_len = row_count * RING, col_count * RING
    c_shape = (COL_CHUNKS, col_len, col_step, HEAD_DIM)
    r_shape = (row_count, row_len, HEAD_DIM)
    flat = (col_len * col_step, HEAD_DIM)
    dma = pltpu.SemaphoreType.DMA
    scratch = [
        pltpu.VMEM((4, *c_shape), BF16),
        pltpu.VMEM((2, *c_shape), BF16),
        pltpu.VMEM((3, *c_shape), BF16),
        pltpu.VMEM((2, *c_shape), BF16),
        pltpu.VMEM((2, *c_shape), BF16),
        pltpu.VMEM((6, *flat), F32),
        pltpu.VMEM((COL_CHUNKS, 5, *flat), F32),
        pltpu.VMEM((4, *r_shape), BF16),
        pltpu.VMEM((2, *r_shape), BF16),
        pltpu.VMEM((3, *r_shape), BF16),
        pltpu.VMEM((2, *r_shape), BF16),
        pltpu.VMEM((2, *r_shape), BF16),
        pltpu.VMEM((2, *r_shape), F32),
    ]
    for chunks in (COL_CHUNKS, ROW_CHUNKS):
        for arrays in (4, 2, 2, 3):
            scratch += [dma((arrays, chunks)), dma((arrays, chunks))]
    scratch += [pltpu.SemaphoreType.REGULAR, pltpu.SemaphoreType.REGULAR]
    shape = jax.ShapeDtypeStruct(queries.shape, BF16)
    grads = pl.pallas_call(
        kernel,
        out_shape=(shape, shape, shape),
        in_specs=[pl.BlockSpec(memory_space=pltpu.HBM)] * 4,
        out_specs=[pl.BlockSpec(memory_space=pl.ANY)] * 3,
        scratch_shapes=scratch,
        compiler_params=pltpu.CompilerParams(
            collective_id=0, has_side_effects=True, vmem_limit_bytes=48 * 2**20
        ),
    )(queries, key_vectors, value_vectors, grad_output)
    return pl.pallas_call(
        hand_out,
        out_shape=(shape, shape, shape),
        in_specs=[pl.BlockSpec(memory_space=pl.ANY)] * 3,
        out_specs=[pl.BlockSpec(memory_space=pltpu.HBM)] * 3,
        scratch_shapes=[dma((3,))],
        compiler_params=pltpu.CompilerParams(vmem_limit_bytes=8 * 2**20),
    )(*grads)


def solution(mesh):
    placed = P("row", "col", None)
    return jax.shard_map(
        body,
        mesh=mesh,
        in_specs=(placed,) * 4,
        out_specs=(placed,) * 3,
        check_vma=False,
    )
```

```python
import functools
import math

import jax
import jax.numpy as jnp
from jax import lax
from jax.experimental import pallas as pl
from jax.experimental.pallas import tpu as pltpu
from jax.sharding import PartitionSpec as P

MESH = pl.DeviceIdType.MESH
HEAD_DIM = 128
RING = 8
FACTOR = 1.0 / math.sqrt(HEAD_DIM)
LOG2E = math.log2(math.e)
BF16, F32 = jnp.bfloat16, jnp.float32

KEY, VALUE, QUERY, GRAD = range(4)
DKEY, DVALUE, DQUERY = range(3)
COL_CHUNKS = 2
ROW_CHUNKS = 2


def attend_back(keys, values, queries, grads, causal_from):
    key_count, query_count = keys.shape[0], queries.shape[0]
    contract_last = (((1,), (1,)), ((), ()))
    raw = lax.dot_general(keys, queries, contract_last, preferred_element_type=F32)
    key_at = lax.broadcasted_iota(jnp.int32, (key_count, query_count), 0)
    query_at = lax.broadcasted_iota(jnp.int32, (key_count, query_count), 1)
    raw = jnp.where(key_at <= query_at + causal_from, raw, -jnp.inf)
    highest = jnp.max(raw, axis=0, keepdims=True)
    weights = jnp.exp2((raw - highest) * (FACTOR * LOG2E))
    probs = weights * (1.0 / jnp.sum(weights, axis=0, keepdims=True))
    probs_low = probs.astype(BF16)
    grad_weights = lax.dot_general(values, grads, contract_last, preferred_element_type=F32)
    correction = jnp.sum(probs_low.astype(F32) * grad_weights, axis=0, keepdims=True)
    grad_scores = (probs * (grad_weights - correction)).astype(BF16)
    grad_values = jnp.dot(probs_low, grads, preferred_element_type=F32)
    grad_keys = jnp.dot(grad_scores, queries, preferred_element_type=F32) * FACTOR
    grad_queries = (
        lax.dot_general(grad_scores, keys, (((0,), (0,)), ((), ())), preferred_element_type=F32)
        * FACTOR
    )
    return grad_keys, grad_values, grad_queries


def kernel(
    q_ref, k_ref, v_ref, g_ref, dq_ref, dk_ref, dv_ref,
    c_in, c_low, c_out, c_part, c_back, f_in, f_out,
    r_in, r_low, r_out, r_part, r_back, r_sum,
    ci_send, ci_recv, cl_send, cl_recv, cb_send, cb_recv, co_send, co_recv,
    ri_send, ri_recv, rl_send, rl_recv, rb_send, rb_recv, ro_send, ro_recv, ring_sem, go_sem,
):
    inputs = (k_ref, v_ref, q_ref, g_ref)
    outputs = (dk_ref, dv_ref, dq_ref)
    row_count, col_count, width = q_ref.shape
    half = width // 2
    col_step = col_count // COL_CHUNKS
    row_step = row_count // ROW_CHUNKS
    col_len = row_count * RING
    row_len = col_count * RING

    row = lax.axis_index("row")
    col = lax.axis_index("col")
    x_lo, z = row // RING, lax.rem(row, RING)
    x_hi, j = col // RING, lax.rem(col, RING)

    def z_peer(at):
        return (x_lo * RING + at, col)

    def j_peer(at):
        return (row, x_hi * RING + at)

    lo_peer = ((1 - x_lo) * RING + z, col)
    hi_peer = (row, (1 - x_hi) * RING + j)

    def others(start, step):
        def at(d, carry):
            step(lax.rem(start + d, RING))
            return carry

        lax.fori_loop(1, RING, at, 0)

    barrier = pltpu.get_barrier_semaphore()

    def signal(sem, target):
        pl.semaphore_signal(sem, inc=1, device_id=target, device_id_type=MESH)

    def signal_rings(sem):
        others(j, lambda at: signal(sem, j_peer(at)))
        signal(sem, lo_peer)
        signal(sem, hi_peer)

    others(z, lambda at: signal(barrier, z_peer(at)))

    @pl.when(z == 0)
    def _():
        signal_rings(barrier)
        pl.semaphore_wait(barrier, RING - 1 + RING + 1)

    @pl.when(z != 0)
    def _():
        pl.semaphore_wait(barrier, RING - 1)

    def lanes(first):
        return pl.ds(pl.multiple_of(first, HEAD_DIM), HEAD_DIM)

    def send(src, dst, send_sem, recv_sem, target):
        pltpu.make_async_remote_copy(
            src_ref=src, dst_ref=dst, send_sem=send_sem, recv_sem=recv_sem,
            device_id=target, device_id_type=MESH,
        ).start()

    def take(ref, sem):
        pltpu.make_async_copy(ref, ref, sem).wait()

    def c_rows(at):
        return pl.ds(at * row_count, row_count)

    def r_cols(at):
        return pl.ds(pl.multiple_of(at * col_count, col_count), col_count)

    def c_send_in(t, n):
        def src(at):
            return inputs[t].at[:, pl.ds(n * col_step, col_step), lanes(half + at * HEAD_DIM)]

        dst = c_in.at[t, n, c_rows(z)]
        others(z, lambda at: send(src(at), dst, ci_send.at[t, n], ci_recv.at[t, n], z_peer(at)))
        pltpu.make_async_copy(src(z), dst, ci_recv.at[t, n]).start()

    def c_send_out(tensors, n, order):
        def one(o, at):
            src = c_out.at[o, n, c_rows(at)]
            dst = outputs[o].at[:, pl.ds(n * col_step, col_step), lanes(half + z * HEAD_DIM)]

            @pl.when(at != z)
            def _():
                send(src, dst, co_send.at[o, n], co_recv.at[o, n], z_peer(at))

            @pl.when(at == z)
            def _():
                pltpu.make_async_copy(src, dst, co_recv.at[o, n]).start()

        def step(i, carry):
            for o in tensors:
                one(o, order(i))
            return carry

        lax.fori_loop(0, RING, step, 0)

    def round_from_here(i):
        return lax.rem(z + i, RING)

    def early_first(i):
        later = RING // 2 + lax.rem(z + i // 2, RING // 2)
        return jnp.where(lax.rem(i, 2) == 0, i // 2, later)

    def r_span(n):
        return pl.ds(n * row_step, row_step)

    def r_send_in(t, n):
        def src(at):
            return inputs[t].at[r_span(n), :, lanes(at * HEAD_DIM)]

        dst = r_in.at[t, r_span(n), r_cols(j)]
        others(j, lambda at: send(src(at), dst, ri_send.at[t, n], ri_recv.at[t, n], j_peer(at)))
        pltpu.make_async_copy(src(j), dst, ri_recv.at[t, n]).start()

    def r_send_out(o, n):
        dst = outputs[o].at[r_span(n), :, lanes(j * HEAD_DIM)]

        def src(at):
            return r_out.at[o, r_span(n), r_cols(at)]

        others(j, lambda at: send(src(at), dst, ro_send.at[o, n], ro_recv.at[o, n], j_peer(at)))
        pltpu.make_async_copy(src(j), dst, ro_recv.at[o, n]).start()

    def c_relay(n):
        @pl.when(x_lo == 0)
        def _():
            for t in (KEY, VALUE):
                take(c_in.at[t, n], ci_recv.at[t, n])
                send(c_in.at[t, n], c_low.at[t, n], cl_send.at[t, n], cl_recv.at[t, n], lo_peer)

    def r_relay(n):
        @pl.when(x_hi == 0)
        def _():
            for t in (KEY, VALUE):
                take(r_in.at[t, r_span(n)], ri_recv.at[t, n])
                send(
                    r_in.at[t, r_span(n)], r_low.at[t, r_span(n)],
                    rl_send.at[t, n], rl_recv.at[t, n], hi_peer,
                )

    def spread(slot, ref):
        f_in[slot, : col_len * col_step] = ref[...].astype(F32).reshape(-1, HEAD_DIM)

    def packed(n, slot):
        return f_out[n, slot, : col_len * col_step].reshape(col_len, col_step, HEAD_DIM)

    def c_work(n):
        def column(slot, c):
            return f_in[slot, pl.ds(c, col_len, stride=col_step), :].astype(BF16)

        def put(slot, c, value):
            f_out[n, slot, pl.ds(c, col_len, stride=col_step), :] = value

        @pl.when(x_lo == 0)
        def _():
            for t in (KEY, VALUE):
                spread(t, c_in.at[t, n])
            for t in (QUERY, GRAD):
                take(c_in.at[t, n], ci_recv.at[t, n])
                spread(t, c_in.at[t, n])

            def item(c, carry):
                parts = attend_back(
                    column(KEY, c), column(VALUE, c), column(QUERY, c), column(GRAD, c), 0
                )
                for o in range(3):
                    put(o, c, parts[o])
                return carry

            lax.fori_loop(0, col_step, item, 0, unroll=4)
            c_out[DQUERY, n] = packed(n, DQUERY).astype(BF16)
            c_send_out((DQUERY,), n, round_from_here)

        @pl.when(x_lo == 1)
        def _():
            for t in (KEY, VALUE):
                take(c_in.at[t, n], ci_recv.at[t, n])
                spread(t, c_in.at[t, n])
                take(c_low.at[t, n], cl_recv.at[t, n])
                spread(4 + t, c_low.at[t, n])
            for t in (QUERY, GRAD):
                take(c_in.at[t, n], ci_recv.at[t, n])
                spread(t, c_in.at[t, n])

            def item(c, carry):
                keys = jnp.concatenate([column(4 + KEY, c), column(KEY, c)], axis=0)
                values = jnp.concatenate([column(4 + VALUE, c), column(VALUE, c)], axis=0)
                parts = attend_back(keys, values, column(QUERY, c), column(GRAD, c), col_len)
                put(DQUERY, c, parts[DQUERY])
                for o in (DKEY, DVALUE):
                    put(o, c, parts[o][col_len:])
                    put(3 + o, c, parts[o][:col_len])
                return carry

            lax.fori_loop(0, col_step, item, 0, unroll=4)
            for o in (DKEY, DVALUE):
                c_part[o, n] = packed(n, 3 + o).astype(BF16)
                send(c_part.at[o, n], c_back.at[o, n], cb_send.at[o, n], cb_recv.at[o, n], lo_peer)
            for o in (DQUERY, DKEY, DVALUE):
                c_out[o, n] = packed(n, o).astype(BF16)
                last = n == 1 and o == DVALUE
                c_send_out((o,), n, early_first if last else round_from_here)

    def c_finish(n):
        @pl.when(x_lo == 0)
        def _():
            for o in (DKEY, DVALUE):
                take(c_back.at[o, n], cb_recv.at[o, n])
                c_out[o, n] = (packed(n, o) + c_back[o, n].astype(F32)).astype(BF16)
                last = n == 1 and o == DVALUE
                c_send_out((o,), n, early_first if last else round_from_here)

    tile = row_len // 2

    def r_work(n):
        first = n * row_step

        @pl.when(x_hi == 0)
        def _():
            for t in (QUERY, GRAD):
                take(r_in.at[t, r_span(n)], ri_recv.at[t, n])

            def item(i, carry):
                at = first + i
                for o in (DKEY, DVALUE):
                    r_sum[o, at, tile:] = jnp.zeros((tile, HEAD_DIM), F32)
                for part in range(2):
                    seen = (part + 1) * tile
                    span = slice(part * tile, seen)
                    parts = attend_back(
                        r_in[KEY, at, :seen], r_in[VALUE, at, :seen],
                        r_in[QUERY, at, span], r_in[GRAD, at, span], part * tile,
                    )
                    for o in (DKEY, DVALUE):
                        if part == 0:
                            r_sum[o, at, :seen] = parts[o]
                        else:
                            r_sum[o, at, :seen] += parts[o]
                    r_out[DQUERY, at, span] = parts[DQUERY].astype(BF16)
                return carry

            lax.fori_loop(0, row_step, item, 0)
            r_send_out(DQUERY, n)

        @pl.when(x_hi == 1)
        def _():
            for t in range(4):
                take(r_in.at[t, r_span(n)], ri_recv.at[t, n])
            for t in (KEY, VALUE):
                take(r_low.at[t, r_span(n)], rl_recv.at[t, n])

            def item(i, carry):
                at = first + i
                sums = []
                for part in range(2):
                    seen = (part + 1) * tile
                    span = slice(part * tile, seen)
                    keys = jnp.concatenate([r_low[KEY, at], r_in[KEY, at, :seen]], axis=0)
                    values = jnp.concatenate([r_low[VALUE, at], r_in[VALUE, at, :seen]], axis=0)
                    parts = attend_back(
                        keys, values, r_in[QUERY, at, span], r_in[GRAD, at, span],
                        row_len + part * tile,
                    )
                    r_out[DQUERY, at, span] = parts[DQUERY].astype(BF16)
                    sums.append(parts)
                for o in (DKEY, DVALUE):
                    both = row_len + tile
                    total = sums[0][o] + sums[1][o][:both]
                    r_part[o, at] = total[:row_len].astype(BF16)
                    r_out[o, at, :tile] = total[row_len:].astype(BF16)
                    r_out[o, at, tile:] = sums[1][o][both:].astype(BF16)
                return carry

            lax.fori_loop(0, row_step, item, 0)
            for o in (DKEY, DVALUE):
                send(
                    r_part.at[o, r_span(n)], r_back.at[o, r_span(n)],
                    rb_send.at[o, n], rb_recv.at[o, n], hi_peer,
                )
            for o in (DQUERY, DKEY, DVALUE):
                r_send_out(o, n)

    def r_finish(n):
        @pl.when(x_hi == 0)
        def _():
            span = r_span(n)
            for o in (DKEY, DVALUE):
                take(r_back.at[o, span], rb_recv.at[o, n])
                r_out[o, span] = (r_sum[o, span] + r_back[o, span].astype(F32)).astype(BF16)
                r_send_out(o, n)

    for t in (KEY, VALUE, QUERY, GRAD):
        c_send_in(t, 0)

    @pl.when(z == 0)
    def _():
        signal_rings(ring_sem)
        pl.semaphore_wait(ring_sem, RING + 1)
        others(z, lambda at: signal(go_sem, z_peer(at)))

    @pl.when(z != 0)
    def _():
        pl.semaphore_wait(go_sem, 1)

    for t in (KEY, VALUE, QUERY, GRAD):
        r_send_in(t, 0)
        c_send_in(t, 1)
    for t in (KEY, VALUE, QUERY, GRAD):
        r_send_in(t, 1)

    c_relay(0)
    r_relay(0)
    r_work(0)
    r_relay(1)
    c_work(0)
    c_relay(1)
    r_work(1)
    r_finish(0)
    c_finish(0)
    c_work(1)
    c_finish(1)
    r_finish(1)

    sent = (RING - 1) * row_count
    sent_cols = (RING - 1) * col_count
    for n in range(2):
        for t in range(4):
            take(c_in.at[t, n, :sent], ci_send.at[t, n])
            take(r_in.at[t, r_span(n), :sent_cols], ri_send.at[t, n])
        for t in (KEY, VALUE):
            @pl.when(x_lo == 0)
            def _():
                take(c_in.at[t, n], cl_send.at[t, n])

            @pl.when(x_lo == 1)
            def _():
                take(c_part.at[t, n], cb_send.at[t, n])

            @pl.when(x_hi == 0)
            def _():
                take(r_in.at[t, r_span(n)], rl_send.at[t, n])

            @pl.when(x_hi == 1)
            def _():
                take(r_part.at[t, r_span(n)], rb_send.at[t, n])
        for o in (DQUERY, DKEY, DVALUE):
            take(r_out.at[o, r_span(n), :sent_cols], ro_send.at[o, n])
            take(r_out.at[o, r_span(n)], ro_recv.at[o, n])
    for n in range(2):
        for o in (DQUERY, DKEY, DVALUE):
            take(c_out.at[o, n, :sent], co_send.at[o, n])
            take(c_out.at[o, n], co_recv.at[o, n])


def hand_out(*refs):
    sems = refs[-1]
    copies = [pltpu.make_async_copy(refs[o], refs[3 + o], sems.at[o]) for o in range(3)]
    for copy in copies:
        copy.start()
    for copy in copies:
        copy.wait()


def body(queries, key_vectors, value_vectors, grad_output):
    row_count, col_count, width = queries.shape
    col_step = col_count // COL_CHUNKS
    col_len, row_len = row_count * RING, col_count * RING
    c_shape = (COL_CHUNKS, col_len, col_step, HEAD_DIM)
    r_shape = (row_count, row_len, HEAD_DIM)
    flat = (col_len * col_step + col_step, HEAD_DIM)
    dma = pltpu.SemaphoreType.DMA
    scratch = [
        pltpu.VMEM((4, *c_shape), BF16),
        pltpu.VMEM((2, *c_shape), BF16),
        pltpu.VMEM((3, *c_shape), BF16),
        pltpu.VMEM((2, *c_shape), BF16),
        pltpu.VMEM((2, *c_shape), BF16),
        pltpu.VMEM((6, *flat), F32),
        pltpu.VMEM((COL_CHUNKS, 5, *flat), F32),
        pltpu.VMEM((4, *r_shape), BF16),
        pltpu.VMEM((2, *r_shape), BF16),
        pltpu.VMEM((3, *r_shape), BF16),
        pltpu.VMEM((2, *r_shape), BF16),
        pltpu.VMEM((2, *r_shape), BF16),
        pltpu.VMEM((2, *r_shape), F32),
    ]
    for chunks in (COL_CHUNKS, ROW_CHUNKS):
        for arrays in (4, 2, 2, 3):
            scratch += [dma((arrays, chunks)), dma((arrays, chunks))]
    scratch += [pltpu.SemaphoreType.REGULAR, pltpu.SemaphoreType.REGULAR]
    shape = jax.ShapeDtypeStruct(queries.shape, BF16)
    grads = pl.pallas_call(
        kernel,
        out_shape=(shape, shape, shape),
        in_specs=[pl.BlockSpec(memory_space=pltpu.HBM)] * 4,
        out_specs=[pl.BlockSpec(memory_space=pl.ANY)] * 3,
        scratch_shapes=scratch,
        compiler_params=pltpu.CompilerParams(
            collective_id=0, has_side_effects=True, vmem_limit_bytes=48 * 2**20
        ),
    )(queries, key_vectors, value_vectors, grad_output)
    return pl.pallas_call(
        hand_out,
        out_shape=(shape, shape, shape),
        in_specs=[pl.BlockSpec(memory_space=pl.ANY)] * 3,
        out_specs=[pl.BlockSpec(memory_space=pltpu.HBM)] * 3,
        scratch_shapes=[dma((3,))],
        compiler_params=pltpu.CompilerParams(vmem_limit_bytes=8 * 2**20),
    )(*grads)


def solution(mesh):
    placed = P("row", "col", None)
    return jax.shard_map(
        body,
        mesh=mesh,
        in_specs=(placed,) * 4,
        out_specs=(placed,) * 3,
        check_vma=False,
    )
```
